256 devices in a mesh: dp: 4 (over y), row: 4 (over x), col: 16 (over z, core).
Axes of the slice: x: 4, y: 4, z: 8, core: 2. Of those that a mesh axis runs over, the one named last changes fastest.
Arguments:
- grad_parts: bfloat16 [4, 7168, 8192], P('dp', 'row', 'col'), may hold values from -350 to 350
- momentum: float32 [4, 1792, 8192], P('row', 'dp', 'col'), may hold values from -700 to 700
- iterate: bfloat16 [7168, 8192], P(('dp', 'row'), 'col'), may hold values from -2.4 to 2.4
Outputs:
- new_momentum: float32 [4, 1792, 8192], P('row', 'dp', 'col')
- start_iterate: float32 [4, 1792, 8192], P('row', 'dp', 'col')
- update: float32 [7168, 8192], P(('dp', 'row'), 'col')
The draws below stay inside these ranges and needn't reach their ends.
All inputs are finite; a program needn't handle non-finite values.
Results may differ from the reference program's by a relative error of at most 0.019.
Values may be sent and summed in bfloat16 or wider, within the bound.
No kernel may reach another device: no remote copies, remote signals or barrier semaphores. Data moves between devices by JAX's collectives and lax.ppermute only.
A program may use at most 64 MiB of HBM per device.

```python
import math
import jax
import jax.numpy as jnp
from jax import lax

R = 7168
C = 8192
N_DP = 4
N_ROW = 4
N_COL = 16


def common_part(key, rank):
    key_left, key_right, key_weight = jax.random.split(key, 3)
    left_vecs = jax.random.truncated_normal(key_left, -4.0, 4.0, (rank, R, 1), jnp.float32)
    right_vecs = jax.random.truncated_normal(key_right, -4.0, 4.0, (rank, 1, C), jnp.float32)
    weights = jnp.exp(jax.random.uniform(key_weight, (rank, 1, 1), jnp.float32, math.log(0.3), 0.0))
    accumulated = jnp.zeros((R, C), jnp.float32)
    for index in range(rank):
        accumulated = accumulated + weights[index] * left_vecs[index] * right_vecs[index]
    return accumulated


def spread_scales(key):
    key_rows, key_cols = jax.random.split(key)
    row_ramp = jnp.exp(math.log(3.0) * jnp.arange(R, dtype=jnp.float32) / (R - 1))
    col_ramp = jnp.exp(math.log(3.0) * jnp.arange(C, dtype=jnp.float32) / (C - 1))
    row_scale = jnp.exp(jax.random.uniform(key_rows, (R,), jnp.float32, 0.0, math.log(10.0))) * row_ramp
    col_scale = jnp.exp(jax.random.uniform(key_cols, (C,), jnp.float32, 0.0, math.log(10.0))) * col_ramp
    return row_scale[:, None] * col_scale[None, :] / 30.0


def draw_grad_parts(key, part):
    key = jax.random.fold_in(key, 11)
    key_common, key_scale, key_noise = jax.random.split(key, 3)
    scales = spread_scales(key_scale)
    shared = common_part(key_common, 8)
    noise = jax.random.truncated_normal(key_noise, -4.0, 4.0, (N_DP, R, C), jnp.float32)
    values = shared[None] + noise * scales[None]
    return values.astype(jnp.bfloat16)


def draw_momentum(key, part):
    key = jax.random.fold_in(key, 23)
    key_common, key_scale, key_noise = jax.random.split(key, 3)
    scales = spread_scales(key_scale)
    shared = common_part(key_common, 8)
    noise = jax.random.truncated_normal(key_noise, -4.0, 4.0, (R, C), jnp.float32)
    values = 2.0 * (shared + noise * scales)
    return values.reshape(N_ROW, R // N_ROW, C)


def draw_iterate(key, part):
    key = jax.random.fold_in(key, 37)
    key_main = jax.random.fold_in(key, 0)
    values = 0.6 * jax.random.truncated_normal(key_main, -3.9, 3.9, (R, C), jnp.float32)
    return values.astype(jnp.bfloat16)


def setup_inputs(seed: int = 0) -> dict:
    key_of = jax.random.split(jax.random.key(seed), 4)
    return {
        "grad_parts": draw_grad_parts(jax.random.fold_in(key_of[3], 71), 0),
        "momentum": draw_momentum(jax.random.fold_in(key_of[3], 71), 0),
        "iterate": draw_iterate(jax.random.fold_in(key_of[3], 71), 0),
    }


def reference(grad_parts, momentum, iterate):
    summed = lax.optimization_barrier(jnp.sum(grad_parts.astype(jnp.float32), axis=0))
    previous = momentum.reshape(R, C)
    new_momentum = 0.95 * previous + summed
    squares = jnp.sum(new_momentum * new_momentum)
    start_iterate = new_momentum * (math.sqrt(R * C) / (jnp.sqrt(squares) + 1e-07))
    group_width = C // N_COL

    def add_group(index, gram_sum):
        begin_col = (index * group_width).astype(jnp.int32)
        column_block = lax.dynamic_slice_in_dim(iterate, begin_col, group_width, 1)
        partial_gram = jnp.dot(column_block, column_block.T, preferred_element_type=jnp.float32) * (1.0 / C)
        rounded = lax.optimization_barrier(partial_gram.astype(jnp.bfloat16))
        return gram_sum + rounded.astype(jnp.float32)
    gram_sum = lax.fori_loop(0, N_COL, add_group, jnp.zeros((R, R), jnp.float32))
    gram = gram_sum.astype(jnp.bfloat16)
    first_product = jnp.dot(gram, iterate, preferred_element_type=jnp.float32)
    first_round = first_product.astype(jnp.bfloat16)
    second_product = jnp.dot(gram, first_round, preferred_element_type=jnp.float32)
    update = 0.2 * (3.4445 * iterate.astype(jnp.float32) - 4.775 * first_product + 2.0315 * second_product)
    return (new_momentum.reshape(N_ROW, R // N_ROW, C), start_iterate.reshape(N_ROW, R // N_ROW, C), update)
```

```python
import math

import jax
import jax.numpy as jnp
from jax import lax
from jax.sharding import Mesh
from jax.sharding import PartitionSpec as P

R = 7168
C = 8192

quintic_a = 3.4445
quintic_b = -4.775
quintic_c = 2.0315

N_DP = 4
N_ROW = 4
N_Z = 8
HALF = 256
contract_last = (((1,), (1,)), ((), ()))
contract_first = (((0,), (0,)), ((), ()))
contract_plain = (((1,), (0,)), ((), ()))


def fetch(value, axis, size, offset):
    return lax.ppermute(value, axis, [((i + offset) % size, i) for i in range(size)])


def swap_cores(value):
    return lax.ppermute(value, "core", [(0, 1), (1, 0)])


def dot(left, right, dims):
    return lax.dot_general(left, right, dims, preferred_element_type=jnp.float32)


def total_of(value):
    value = jnp.broadcast_to(value, (8, 128))
    for axis, size in (("core", 2), ("row", N_ROW), ("dp", N_DP), ("z", N_Z)):
        step = 1
        while step < size:
            other = lax.ppermute(value, axis, [(i ^ step, i) for i in range(size)])
            value = value + other
            step *= 2
    return value[0, 0]


def local(grad_parts, momentum, iterate):
    core = lax.axis_index("core")
    inverse_width = 1.0 / C

    rows_i = jnp.concatenate(
        [iterate] + [fetch(iterate, "row", N_ROW, k) for k in (1, 2, 3)], axis=0
    )
    rows_j = jnp.concatenate(
        [iterate] + [fetch(iterate, "dp", N_DP, k) for k in (1, 2, 3)], axis=0
    )
    half_rows = rows_j.shape[0] // 2

    def mine_and_other(stacked):
        mine = lax.dynamic_slice_in_dim(stacked, core * half_rows, half_rows, 0)
        other = lax.dynamic_slice_in_dim(stacked, (1 - core) * half_rows, half_rows, 0)
        return mine, other

    j_mine, j_other = mine_and_other(rows_j)
    gram_away = (dot(rows_i, j_other, contract_last) * inverse_width).astype(jnp.bfloat16)
    gram_back = swap_cores(gram_away).astype(jnp.float32)
    gram_pair = (dot(rows_i, j_mine, contract_last) * inverse_width + gram_back).astype(
        jnp.bfloat16
    )
    gram_share = lax.psum_scatter(gram_pair, "z", scatter_dimension=0, tiled=True)
    gram_mine = lax.all_gather(gram_share, "z", axis=0, tiled=True)
    gram_other = swap_cores(gram_mine)

    grad_tied, _ = lax.optimization_barrier((grad_parts, gram_away))
    summed = lax.psum_scatter(grad_tied, "dp", scatter_dimension=1, tiled=True).astype(jnp.float32)
    new_momentum = 0.95 * momentum + summed
    squares = total_of(jnp.sum(new_momentum * new_momentum))
    start_iterate = new_momentum * (math.sqrt(R * C) / (jnp.sqrt(squares) + 1e-07))

    def multiply(of_j, of_i):
        mine, other = mine_and_other(of_j)
        part_i = dot(gram_mine, mine, contract_plain) + dot(gram_other, other, contract_plain)
        part_mine = dot(gram_mine, of_i, contract_first)
        part_other = dot(gram_other, of_i, contract_first)
        first = jnp.where(core == 0, part_mine, part_other)
        second = jnp.where(core == 0, part_other, part_mine)
        height = iterate.shape[0]
        blocks_i = [part_i[k * height : (k + 1) * height] for k in range(4)]
        blocks_j = [first[:height], first[height:], second[:height], second[height:]]
        sum_i, sum_j = blocks_i[0], blocks_j[0]
        for k in (1, 2, 3):
            sum_i = sum_i + fetch(blocks_i[k].astype(jnp.bfloat16), "row", N_ROW, -k).astype(
                jnp.float32
            )
            sum_j = sum_j + fetch(blocks_j[k].astype(jnp.bfloat16), "dp", N_DP, -k).astype(
                jnp.float32
            )
        return sum_i, sum_j

    first_a, first_b = multiply(rows_j[:, :HALF], rows_i[:, HALF:])
    round_a, round_b = first_a.astype(jnp.bfloat16), first_b.astype(jnp.bfloat16)
    first_j = jnp.concatenate(
        [round_a] + [fetch(round_a, "dp", N_DP, k) for k in (1, 2, 3)], axis=0
    )
    first_i = jnp.concatenate(
        [round_b] + [fetch(round_b, "row", N_ROW, k) for k in (1, 2, 3)], axis=0
    )
    second_a, second_b = multiply(first_j, first_i)

    first_product = jnp.concatenate([first_a, first_b], axis=1)
    second_product = jnp.concatenate([second_a, second_b], axis=1)
    update = 0.2 * (
        quintic_a * iterate.astype(jnp.float32)
        + quintic_b * first_product
        + quintic_c * second_product
    )
    return (new_momentum, start_iterate, update)


def solution(mesh):
    fine = Mesh(mesh.devices.reshape(N_DP, N_ROW, N_Z, 2), ("dp", "row", "z", "core"))
    in_specs = (
        P("dp", "row", ("z", "core")),
        P("row", "dp", ("z", "core")),
        P(("dp", "row"), ("z", "core")),
    )
    out_specs = (in_specs[1], in_specs[1], in_specs[2])
    return jax.shard_map(local, mesh=fine, in_specs=in_specs, out_specs=out_specs, check_vma=False)
```

```python
import math

import jax
import jax.numpy as jnp
from jax import lax
from jax.sharding import Mesh
from jax.sharding import PartitionSpec as P

R = 7168
C = 8192

quintic_a = 3.4445
quintic_b = -4.775
quintic_c = 2.0315

N_DP = 4
N_ROW = 4
N_Z = 8
contract_last = (((1,), (1,)), ((), ()))
contract_plain = (((1,), (0,)), ((), ()))
contract_first = (((0,), (0,)), ((), ()))


def side_pairs(side, offsets):
    pairs = []
    for d in range(N_DP):
        for r in range(N_ROW):
            for c in range(2):
                offset = offsets[c]
                along_row = (c == 0) == (side == "out")
                source_d = d if along_row else (d + offset) % N_DP
                source_r = (r + offset) % N_ROW if along_row else r
                pairs.append(((source_d * N_ROW + source_r) * 2 + c, (d * N_ROW + r) * 2 + c))
    return pairs


def fetch_by_core(value, side, offsets):
    return lax.ppermute(value, ("dp", "row", "core"), side_pairs(side, offsets))


def fetch_side(value, side, offset):
    return fetch_by_core(value, side, (offset, offset))


def fetch(value, axis, size, offset):
    return lax.ppermute(value, axis, [((i + offset) % size, i) for i in range(size)])


def swap_cores(value):
    return lax.ppermute(value, "core", [(0, 1), (1, 0)])


def dot(left, right, dims):
    return lax.dot_general(left, right, dims, preferred_element_type=jnp.float32)


def exchange_sum(value, axis, size, step):
    return value + lax.ppermute(value, axis, [(i ^ step, i) for i in range(size)])


EXCHANGES = (
    ("core", 2, 1),
    ("row", N_ROW, 1),
    ("row", N_ROW, 2),
    ("dp", N_DP, 1),
    ("dp", N_DP, 2),
    ("z", N_Z, 1),
    ("z", N_Z, 2),
    ("z", N_Z, 4),
)


def after(value, *others):
    return lax.optimization_barrier((value,) + others)[0]


def gather_side(value, side):
    half = value.shape[0] // 2
    ahead = fetch_side(value, side, 1)
    behind = fetch_side(value, side, -1)
    top = fetch_side(ahead[:half], side, 1)
    bottom = fetch_side(behind[half:], side, -1)
    return [value, ahead, jnp.concatenate([top, bottom], axis=0), behind]


def local(grad_parts, momentum, iterate):
    core = lax.axis_index("core")
    height = iterate.shape[0]
    inverse_width = 1.0 / C

    def by_core(for_first, for_second):
        return jnp.where(core == 0, for_first, for_second)

    out_blocks = gather_side(iterate, "out")
    in_blocks = gather_side(iterate, "in")
    own_swapped = swap_cores(iterate)
    out_other = [own_swapped] + [swap_cores(block) for block in in_blocks[1:]]
    in_other = [own_swapped] + [swap_cores(block) for block in out_blocks[1:]]

    def pair(blocks, k):
        return jnp.concatenate(blocks[2 * k : 2 * k + 2], axis=0)

    x_in = [pair(in_blocks, t) for t in range(2)]
    x_in_other = [pair(in_other, t) for t in range(2)]
    shares = []
    for t in range(2):
        rows = by_core(pair(out_blocks, t), pair(out_blocks, 1 - t))
        rows_other = by_core(pair(out_other, t), pair(out_other, 1 - t))
        part = dot(rows, x_in[t], contract_last) + dot(rows_other, x_in_other[t], contract_last)
        part = (part * inverse_width).astype(jnp.bfloat16)
        if t == 0:
            tied = after(grad_parts, part)
        shares.append(lax.psum_scatter(part, "z", scatter_dimension=0, tiled=True))

    place_dp = lax.axis_index("dp")
    rows_of = [
        lax.dynamic_slice_in_dim(tied, lax.rem(place_dp + k, N_DP) * height, height, 1)
        for k in range(N_DP)
    ]
    summed = rows_of[0].astype(jnp.float32)
    for k in (1, 2, 3):
        summed = summed + fetch(rows_of[k], "dp", N_DP, -k).astype(jnp.float32)
    new_momentum = 0.95 * momentum + summed
    squares = jnp.broadcast_to(jnp.sum(new_momentum * new_momentum), (8, 128))
    shares[0] = after(shares[0], squares)
    for axis, size, step in EXCHANGES:
        squares = exchange_sum(squares, axis, size, step)

    slots = [lax.all_gather(share, "z", axis=0, tiled=True) for share in shares]
    slots[0] = after(slots[0], squares)
    arrived = [swap_cores(slot) for slot in slots]
    scale = math.sqrt(R * C) / (jnp.sqrt(squares[0, 0]) + 1e-07)
    start_iterate = new_momentum * scale
    turned = [by_core(arrived[t], arrived[1 - t]) for t in range(2)]

    def multiply(contracted):
        parts = [
            lax.optimization_barrier(dot(slots[t], contracted[t], contract_plain))
            + dot(turned[t], contracted[1 - t], contract_first)
            for t in range(2)
        ]
        total = by_core(parts[0][:height], parts[1][:height])
        far = by_core(parts[1][:height], parts[0][:height]).astype(jnp.bfloat16)
        odd = [part[height:].astype(jnp.bfloat16) for part in parts]
        arrived = [fetch_side(far, "out", 2)]
        arrived += [fetch_by_core(odd[0], "out", (-1, 1)), fetch_by_core(odd[1], "out", (1, -1))]
        for value in arrived:
            total = total + value.astype(jnp.float32)
        return total

    first_product = multiply(x_in)
    rounded = first_product.astype(jnp.bfloat16)
    first_in = [rounded] + [fetch_side(rounded, "in", k) for k in (1, 2, 3)]
    second_product = multiply([pair(first_in, t) for t in range(2)])

    update = 0.2 * (
        quintic_a * iterate.astype(jnp.float32)
        + quintic_b * first_product
        + quintic_c * second_product
    )
    return (new_momentum, start_iterate, update)


def solution(mesh):
    fine = Mesh(mesh.devices.reshape(N_DP, N_ROW, N_Z, 2), ("dp", "row", "z", "core"))
    in_specs = (
        P("dp", "row", ("z", "core")),
        P("row", "dp", ("z", "core")),
        P(("dp", "row"), ("z", "core")),
    )
    out_specs = (in_specs[1], in_specs[1], in_specs[2])
    return jax.shard_map(local, mesh=fine, in_specs=in_specs, out_specs=out_specs, check_vma=False)
```

```python
import math

import jax
import jax.numpy as jnp
from jax import lax
from jax.sharding import Mesh
from jax.sharding import PartitionSpec as P

R = 7168
C = 8192

quintic_a = 3.4445
quintic_b = -4.775
quintic_c = 2.0315

N_DP = 4
N_ROW = 4
N_Z = 8
contract_last = (((1,), (1,)), ((), ()))
contract_plain = (((1,), (0,)), ((), ()))
contract_first = (((0,), (0,)), ((), ()))


def side_pairs(side, offsets):
    pairs = []
    for d in range(N_DP):
        for r in range(N_ROW):
            for c in range(2):
                offset = offsets[c]
                along_row = (c == 0) == (side == "out")
                source_d = d if along_row else (d + offset) % N_DP
                source_r = (r + offset) % N_ROW if along_row else r
                pairs.append(((source_d * N_ROW + source_r) * 2 + c, (d * N_ROW + r) * 2 + c))
    return pairs


def fetch_by_core(value, side, offsets):
    return lax.ppermute(value, ("dp", "row", "core"), side_pairs(side, offsets))


def fetch_side(value, side, offset):
    return fetch_by_core(value, side, (offset, offset))


def fetch(value, axis, size, offset):
    return lax.ppermute(value, axis, [((i + offset) % size, i) for i in range(size)])


def swap_cores(value):
    return lax.ppermute(value, "core", [(0, 1), (1, 0)])


def dot(left, right, dims):
    return lax.dot_general(left, right, dims, preferred_element_type=jnp.float32)


def exchange_sum(value, axis, size, step):
    return value + lax.ppermute(value, axis, [(i ^ step, i) for i in range(size)])


EXCHANGES = (
    ("core", 2, 1),
    ("row", N_ROW, 1),
    ("row", N_ROW, 2),
    ("dp", N_DP, 1),
    ("dp", N_DP, 2),
    ("z", N_Z, 1),
    ("z", N_Z, 2),
    ("z", N_Z, 4),
)


def after(value, *others):
    return lax.optimization_barrier((value,) + others)[0]


def gather_side(value, side):
    ahead = fetch_side(value, side, 1)
    behind = fetch_side(value, side, -1)
    opposite = fetch_side(ahead, side, 1) if side == "out" else fetch_side(behind, side, -1)
    return [value, ahead, opposite, behind]


def ring_fetch(value):
    pairs = [
        (((z + (-1 if c == 0 else 1)) % N_Z) * 2 + c, z * 2 + c) for z in range(N_Z) for c in range(2)
    ]
    return lax.ppermute(value, ("z", "core"), pairs)


OUT_GROUPS = [[(d * N_ROW + r) * 2 for r in range(N_ROW)] for d in range(N_DP)] + [
    [(d * N_ROW + r) * 2 + 1 for d in range(N_DP)] for r in range(N_ROW)
]


def local(grad_parts, momentum, iterate):
    core = lax.axis_index("core")
    height = iterate.shape[0]
    inverse_width = 1.0 / C

    place_z = lax.axis_index("z")
    shard = 2 * height // N_Z

    def place(steps):
        return lax.rem(place_z + steps * (1 - 2 * core) + N_Z, N_Z)

    def ring_sum(part):
        def rows(steps):
            return lax.dynamic_slice_in_dim(part, place(steps) * shard, shard, 0)

        moving = rows(N_Z - 1).astype(jnp.bfloat16)
        for steps in range(N_Z - 2, -1, -1):
            moving = (rows(steps) + ring_fetch(moving).astype(jnp.float32)).astype(jnp.bfloat16)
        return moving

    def by_core(for_first, for_second):
        return jnp.where(core == 0, for_first, for_second)

    out_blocks = gather_side(iterate, "out")
    in_blocks = gather_side(iterate, "in")
    own_swapped = swap_cores(iterate)
    out_other = [own_swapped] + [swap_cores(block) for block in in_blocks[1:]]
    in_other = [own_swapped] + [swap_cores(block) for block in out_blocks[1:]]

    def pair(blocks, k):
        return jnp.concatenate(blocks[2 * k : 2 * k + 2], axis=0)

    x_in = [pair(in_blocks, t) for t in range(2)]
    x_in_other = [pair(in_other, t) for t in range(2)]
    shares = []
    for t in range(2):
        rows = by_core(pair(out_blocks, t), pair(out_blocks, 1 - t))
        rows_other = by_core(pair(out_other, t), pair(out_other, 1 - t))
        part = dot(rows, x_in[t], contract_last) + dot(rows_other, x_in_other[t], contract_last)
        part = part * inverse_width
        if t == 0:
            tied = after(grad_parts, part)
        shares.append(ring_sum(part))

    place_dp = lax.axis_index("dp")
    rows_of = [
        lax.dynamic_slice_in_dim(tied, lax.rem(place_dp + k, N_DP) * height, height, 1)
        for k in range(N_DP)
    ]
    summed = rows_of[0].astype(jnp.float32)
    for k in (1, 2, 3):
        summed = summed + fetch(rows_of[k], "dp", N_DP, -k).astype(jnp.float32)
    new_momentum = 0.95 * momentum + summed
    squares = jnp.broadcast_to(jnp.sum(new_momentum * new_momentum), (8, 128))
    shares[0] = after(shares[0], squares)

    slots = [jnp.zeros((2 * height, 2 * height), jnp.bfloat16) for _ in range(2)]
    arrived = [jnp.zeros((2 * height, 2 * height), jnp.bfloat16) for _ in range(2)]
    moving = jnp.concatenate(shares, axis=0)
    for step in range(N_Z):
        if step > 0:
            moving = ring_fetch(moving)
            axis, size, distance = EXCHANGES[step - 1]
            squares = exchange_sum(after(squares, moving), axis, size, distance)
        swapped = swap_cores(moving)
        for t in range(2):
            for buffers, value, at in ((slots, moving, -step), (arrived, swapped, step)):
                buffers[t] = lax.dynamic_update_slice_in_dim(
                    buffers[t], value[t * shard : (t + 1) * shard], place(at) * shard, 0
                )
    slots[0] = after(slots[0], squares)
    squares = exchange_sum(squares, *EXCHANGES[-1])
    scale = math.sqrt(R * C) / (jnp.sqrt(squares[0, 0]) + 1e-07)
    start_iterate = new_momentum * scale
    turned = [by_core(arrived[t], arrived[1 - t]) for t in range(2)]

    me = by_core(lax.axis_index("row"), lax.axis_index("dp"))

    def multiply(contracted):
        parts = [
            lax.optimization_barrier(dot(slots[t], contracted[t], contract_plain))
            + dot(turned[t], contracted[1 - t], contract_first)
            for t in range(2)
        ]
        total = by_core(parts[0][:height], parts[1][:height])
        stacked = jnp.concatenate(parts, axis=0).astype(jnp.bfloat16)
        away = jnp.concatenate(
            [
                lax.dynamic_slice_in_dim(stacked, lax.rem(k - me + 4 + 2 * core, 4) * height, height, 0)
                for k in range(4)
            ],
            axis=0,
        )
        back = lax.all_to_all(
            away, ("dp", "row", "core"), 0, 0, axis_index_groups=OUT_GROUPS, tiled=True
        )
        for k in range(4):
            block = back[k * height : (k + 1) * height].astype(jnp.float32)
            total = total + jnp.where(me == k, 0.0, block)
        return total

    first_product = multiply(x_in)
    rounded = first_product.astype(jnp.bfloat16)
    first_in = [rounded] + [fetch_side(rounded, "in", k) for k in (1, 2, 3)]
    second_product = multiply([pair(first_in, t) for t in range(2)])

    update = 0.2 * (
        quintic_a * iterate.astype(jnp.float32)
        + quintic_b * first_product
        + quintic_c * second_product
    )
    return (new_momentum, start_iterate, update)


def solution(mesh):
    fine = Mesh(mesh.devices.reshape(N_DP, N_ROW, N_Z, 2), ("dp", "row", "z", "core"))
    in_specs = (
        P("dp", "row", ("z", "core")),
        P("row", "dp", ("z", "core")),
        P(("dp", "row"), ("z", "core")),
    )
    out_specs = (in_specs[1], in_specs[1], in_specs[2])
    return jax.shard_map(local, mesh=fine, in_specs=in_specs, out_specs=out_specs, check_vma=False)
```

```python
import math

import jax
import jax.numpy as jnp
from jax import lax
from jax.sharding import Mesh
from jax.sharding import PartitionSpec as P

R = 7168
C = 8192

quintic_a = 3.4445
quintic_b = -4.775
quintic_c = 2.0315

N_DP = 4
N_ROW = 4
N_Z = 8
HALF = 256
contract_last = (((1,), (1,)), ((), ()))
contract_first = (((0,), (0,)), ((), ()))
contract_plain = (((1,), (0,)), ((), ()))


def fetch(value, axis, size, offset):
    return lax.ppermute(value, axis, [((i + offset) % size, i) for i in range(size)])


def swap_cores(value):
    return lax.ppermute(value, "core", [(0, 1), (1, 0)])


def dot(left, right, dims):
    return lax.dot_general(left, right, dims, preferred_element_type=jnp.float32)


def exchange_sum(value, axis, size, step):
    return value + lax.ppermute(value, axis, [(i ^ step, i) for i in range(size)])


def after(value, *others):
    return lax.optimization_barrier((value,) + others)[0]


def gather_two_ways(value, axis):
    half = value.shape[0] // 2
    ahead = fetch(value, axis, 4, 1)
    behind = fetch(value, axis, 4, -1)
    top = fetch(ahead[:half], axis, 4, 1)
    bottom = fetch(behind[half:], axis, 4, -1)
    return [value, ahead, jnp.concatenate([top, bottom], axis=0), behind]


def local(grad_parts, momentum, iterate):
    core = lax.axis_index("core")
    place_z = lax.axis_index("z")
    height = iterate.shape[0]
    shard = 4 * height // N_Z
    inverse_width = 1.0 / C

    def by_core(for_first, for_second):
        return jnp.where(core == 0, for_first, for_second)

    def stack(blocks):
        return jnp.concatenate(blocks, axis=0)

    def own_half(blocks):
        return stack([by_core(blocks[1], blocks[3]), by_core(blocks[0], blocks[2])])

    def other_half(blocks):
        return stack([by_core(blocks[3], blocks[1]), by_core(blocks[2], blocks[0])])

    blocks_i = gather_two_ways(iterate, "row")
    blocks_j = gather_two_ways(iterate, "dp")
    rows_i, rows_i_other = stack(blocks_i), stack([swap_cores(block) for block in blocks_i])
    rows_j = own_half(blocks_j)
    rows_j_other = stack(
        [
            swap_cores(by_core(blocks_j[3], blocks_j[1])),
            swap_cores(by_core(blocks_j[2], blocks_j[0])),
        ]
    )
    part = (
        dot(rows_i, rows_j, contract_last) + dot(rows_i_other, rows_j_other, contract_last)
    ) * inverse_width

    def place(offset):
        return lax.rem(place_z + (offset + N_Z), N_Z) * shard

    def rows_of_shard(offset):
        return lax.dynamic_slice_in_dim(part, place(offset), shard, 0)

    def up(value):
        return fetch(value, "z", N_Z, -1)

    def down(value):
        return fetch(value, "z", N_Z, 1)

    half = shard // 2
    opposite = rows_of_shard(4).astype(jnp.bfloat16)
    rising = up(opposite[:half]).astype(jnp.float32)
    falling = down(opposite[half:]).astype(jnp.float32)
    zeros = jnp.zeros((half, part.shape[1]), jnp.float32)
    tied = after(grad_parts, rising)
    rising = stack([rising, zeros])
    falling = stack([zeros, falling])
    for offset in (3, 2, 1):
        rising, falling = lax.optimization_barrier(
            (
                (rows_of_shard(offset) + rising).astype(jnp.bfloat16),
                (rows_of_shard(-offset) + falling).astype(jnp.bfloat16),
            )
        )
        rising, falling = up(rising).astype(jnp.float32), down(falling).astype(jnp.float32)
    share = (rows_of_shard(0) + rising + falling).astype(jnp.bfloat16)

    place_dp = lax.axis_index("dp")
    rows_of = [
        lax.dynamic_slice_in_dim(tied, lax.rem(place_dp + k, N_DP) * height, height, 1)
        for k in range(N_DP)
    ]
    summed = rows_of[0].astype(jnp.float32)
    for k in (1, 2, 3):
        summed = summed + fetch(rows_of[k], "dp", N_DP, -k).astype(jnp.float32)
    new_momentum = 0.95 * momentum + summed
    squares = jnp.broadcast_to(jnp.sum(new_momentum * new_momentum), (8, 128))

    gram_mine = jnp.zeros(part.shape, jnp.bfloat16)
    gram_other = jnp.zeros(part.shape, jnp.bfloat16)

    def put(value, begin):
        return (
            lax.dynamic_update_slice_in_dim(gram_mine, value, begin, 0),
            lax.dynamic_update_slice_in_dim(gram_other, swap_cores(value), begin, 0),
        )

    gram_mine, gram_other = put(share, place(0))
    rising = falling = share
    for step in (1, 2, 3):
        rising, falling = lax.optimization_barrier((up(rising), down(falling)))
        if step == 2:
            rising = after(rising, squares)
        gram_mine, gram_other = put(rising, place(-step))
        gram_mine, gram_other = put(falling, place(step))
    opposite = stack([up(rising[:half]), down(falling[half:])])
    gram_mine, gram_other = put(opposite, place(4))
    squares = after(squares, gram_mine)

    def multiply(of_j, of_i, squares, exchanges):
        part_i = dot(gram_mine, own_half(of_j), contract_plain) + dot(
            gram_other, other_half(of_j), contract_plain
        )
        sent_i = [fetch(part_i[k * height : (k + 1) * height].astype(jnp.bfloat16), "row", N_ROW, -k) for k in (1, 2, 3)]
        rows_i = stack(of_i)
        mine = dot(gram_mine, rows_i, contract_first)
        other = dot(gram_other, rows_i, contract_first)
        part_j = {
            0: by_core(mine[height:], other[height:]),
            1: by_core(mine[:height], other[:height]),
            2: by_core(other[height:], mine[height:]),
            3: by_core(other[:height], mine[:height]),
        }
        sent_j = [fetch(part_j[k].astype(jnp.bfloat16), "dp", N_DP, -k) for k in (1, 2, 3)]
        squares = after(squares, part_j[0])
        for exchange in exchanges:
            squares = exchange_sum(squares, *exchange)
        sum_i, sum_j = part_i[:height], part_j[0]
        for got_i, got_j in zip(sent_i, sent_j):
            sum_i = sum_i + got_i.astype(jnp.float32)
            sum_j = sum_j + got_j.astype(jnp.float32)
        return sum_i, sum_j, squares

    first_a, first_b, squares = multiply(
        [block[:, :HALF] for block in blocks_j],
        [block[:, HALF:] for block in blocks_i],
        squares,
        (("core", 2, 1), ("z", N_Z, 1), ("z", N_Z, 2), ("z", N_Z, 4)),
    )
    round_a, round_b = first_a.astype(jnp.bfloat16), first_b.astype(jnp.bfloat16)
    first_j = [round_a] + [fetch(round_a, "dp", N_DP, k) for k in (1, 2, 3)]
    first_i = [round_b] + [fetch(round_b, "row", N_ROW, k) for k in (1, 2, 3)]
    first_i[0] = after(first_i[0], squares)
    second_a, second_b, squares = multiply(
        first_j,
        first_i,
        squares,
        (("row", N_ROW, 1), ("row", N_ROW, 2), ("dp", N_DP, 1), ("dp", N_DP, 2)),
    )

    scale = math.sqrt(R * C) / (jnp.sqrt(squares[0, 0]) + 1e-07)
    start_iterate = new_momentum * scale
    first_product = jnp.concatenate([first_a, first_b], axis=1)
    second_product = jnp.concatenate([second_a, second_b], axis=1)
    update = 0.2 * (
        quintic_a * iterate.astype(jnp.float32)
        + quintic_b * first_product
        + quintic_c * second_product
    )
    return (new_momentum, start_iterate, update)


def solution(mesh):
    fine = Mesh(mesh.devices.reshape(N_DP, N_ROW, N_Z, 2), ("dp", "row", "z", "core"))
    in_specs = (
        P("dp", "row", ("z", "core")),
        P("row", "dp", ("z", "core")),
        P(("dp", "row"), ("z", "core")),
    )
    out_specs = (in_specs[1], in_specs[1], in_specs[2])
    return jax.shard_map(local, mesh=fine, in_specs=in_specs, out_specs=out_specs, check_vma=False)
```

```python
import math

import jax
import jax.numpy as jnp
from jax import lax
from jax.sharding import Mesh
from jax.sharding import PartitionSpec as P

R = 7168
C = 8192

quintic_a = 3.4445
quintic_b = -4.775
quintic_c = 2.0315

N_DP = 4
N_ROW = 4
N_Z = 8
HALF = 256
contract_last = (((1,), (1,)), ((), ()))
contract_first = (((0,), (0,)), ((), ()))
contract_plain = (((1,), (0,)), ((), ()))


def fetch(value, axis, size, offset):
    return lax.ppermute(value, axis, [((i + offset) % size, i) for i in range(size)])


def swap_cores(value):
    return lax.ppermute(value, "core", [(0, 1), (1, 0)])


def dot(left, right, dims):
    return lax.dot_general(left, right, dims, preferred_element_type=jnp.float32)


def exchange_sum(value, axis, size, step):
    return value + lax.ppermute(value, axis, [(i ^ step, i) for i in range(size)])


def after(value, *others):
    return lax.optimization_barrier((value,) + others)[0]


def gather_two_ways(value, axis):
    half = value.shape[0] // 2
    ahead = fetch(value, axis, 4, 1)
    behind = fetch(value, axis, 4, -1)
    top = fetch(ahead[:half], axis, 4, 1)
    bottom = fetch(behind[half:], axis, 4, -1)
    return [value, ahead, jnp.concatenate([top, bottom], axis=0), behind]


def local(grad_parts, momentum, iterate):
    core = lax.axis_index("core")
    place_z = lax.axis_index("z")
    height = iterate.shape[0]
    shard = 4 * height // N_Z
    inverse_width = 1.0 / C

    def by_core(for_first, for_second):
        return jnp.where(core == 0, for_first, for_second)

    def stack(blocks):
        return jnp.concatenate(blocks, axis=0)

    def own_half(blocks):
        return stack([by_core(blocks[1], blocks[3]), by_core(blocks[0], blocks[2])])

    def other_half(blocks):
        return stack([by_core(blocks[3], blocks[1]), by_core(blocks[2], blocks[0])])

    blocks_i = gather_two_ways(iterate, "row")
    blocks_j = gather_two_ways(iterate, "dp")
    rows_i, rows_i_other = stack(blocks_i), stack([swap_cores(block) for block in blocks_i])
    rows_j = own_half(blocks_j)
    rows_j_other = stack(
        [
            swap_cores(by_core(blocks_j[3], blocks_j[1])),
            swap_cores(by_core(blocks_j[2], blocks_j[0])),
        ]
    )
    def place(offset):
        return lax.rem(place_z + (offset + N_Z), N_Z) * shard

    def rows_of_shard(offset, arrived=()):
        own = lax.dynamic_slice_in_dim(rows_i, place(offset), shard, 0)
        other = lax.dynamic_slice_in_dim(rows_i_other, place(offset), shard, 0)
        own, other = after(own, *arrived), after(other, *arrived)
        part = dot(own, rows_j, contract_last) + dot(other, rows_j_other, contract_last)
        return lax.optimization_barrier(part * inverse_width)

    def up(value):
        return fetch(value, "z", N_Z, -1)

    def down(value):
        return fetch(value, "z", N_Z, 1)

    half = shard // 2
    opposite = rows_of_shard(4).astype(jnp.bfloat16)
    rising, falling = up(opposite[:half]), down(opposite[half:])
    arrived = ()
    zeros = jnp.zeros((half, 2 * height), jnp.float32)
    place_dp = lax.axis_index("dp")
    rows_of = [
        lax.dynamic_slice_in_dim(grad_parts, lax.rem(place_dp + k, N_DP) * height, height, 1)
        for k in range(N_DP)
    ]
    summed = rows_of[0].astype(jnp.float32)
    after_first = (rising, falling)
    rising = stack([rising.astype(jnp.float32), zeros])
    falling = stack([zeros, falling.astype(jnp.float32)])
    for offset, k in ((3, 1), (2, 3), (1, 2)):
        rising, falling, away = lax.optimization_barrier(
            (
                (rows_of_shard(offset, arrived) + rising).astype(jnp.bfloat16),
                (rows_of_shard(-offset, arrived) + falling).astype(jnp.bfloat16),
                rows_of[k],
            )
        )
        rising, falling, away = lax.optimization_barrier(
            (up(rising), down(falling), fetch(away, "dp", N_DP, -k))
        )
        arrived, after_first = after_first, (rising, falling)
        rising, falling = rising.astype(jnp.float32), falling.astype(jnp.float32)
        summed = summed + away.astype(jnp.float32)
    share = (rows_of_shard(0, arrived) + rising + falling).astype(jnp.bfloat16)
    new_momentum = 0.95 * momentum + summed
    squares = jnp.broadcast_to(jnp.sum(new_momentum * new_momentum), (8, 128))

    gram_mine = jnp.zeros((4 * height, 2 * height), jnp.bfloat16)
    gram_other = jnp.zeros((4 * height, 2 * height), jnp.bfloat16)

    def put(value, begin):
        return (
            lax.dynamic_update_slice_in_dim(gram_mine, value, begin, 0),
            lax.dynamic_update_slice_in_dim(gram_other, swap_cores(value), begin, 0),
        )

    gram_mine, gram_other = put(share, place(0))
    rising = falling = share
    for step, exchange in ((1, ("row", N_ROW, 1)), (2, ("row", N_ROW, 2)), (3, ("dp", N_DP, 1))):
        rising, falling, squares = lax.optimization_barrier(
            (up(rising), down(falling), exchange_sum(squares, *exchange))
        )
        gram_mine, gram_other = put(rising, place(-step))
        gram_mine, gram_other = put(falling, place(step))
    opposite = stack([up(rising[:half]), down(falling[half:])])
    gram_mine, gram_other = put(opposite, place(4))
    squares = exchange_sum(squares, "dp", N_DP, 2)
    gram_mine = after(gram_mine, squares)

    def multiply(of_j, of_i, squares, last):
        part_i = dot(gram_mine, own_half(of_j), contract_plain) + dot(
            gram_other, other_half(of_j), contract_plain
        )
        sent_i = [fetch(part_i[k * height : (k + 1) * height].astype(jnp.bfloat16), "row", N_ROW, -k) for k in (1, 2, 3)]
        rows_i = stack(of_i)
        mine = dot(gram_mine, rows_i, contract_first)
        other = dot(gram_other, rows_i, contract_first)
        part_j = {
            0: by_core(mine[height:], other[height:]),
            1: by_core(mine[:height], other[:height]),
            2: by_core(other[height:], mine[height:]),
            3: by_core(other[:height], mine[:height]),
        }
        sent_j = [fetch(part_j[k].astype(jnp.bfloat16), "dp", N_DP, -k) for k in (1, 2, 3)]
        if last:
            squares = after(squares, *[block for block in part_j.values()])
            squares = exchange_sum(exchange_sum(squares, "z", N_Z, 2), "z", N_Z, 4)
        sum_i, sum_j = part_i[:height], part_j[0]
        for got_i, got_j in zip(sent_i, sent_j):
            sum_i = sum_i + got_i.astype(jnp.float32)
            sum_j = sum_j + got_j.astype(jnp.float32)
        return sum_i, sum_j, squares

    first_a, first_b, squares = multiply(
        [block[:, :HALF] for block in blocks_j],
        [block[:, HALF:] for block in blocks_i],
        squares,
        False,
    )
    round_a, round_b = first_a.astype(jnp.bfloat16), first_b.astype(jnp.bfloat16)
    first_j = [round_a] + [fetch(round_a, "dp", N_DP, k) for k in (1, 2, 3)]
    first_i = [round_b] + [fetch(round_b, "row", N_ROW, k) for k in (1, 2, 3)]
    squares = after(squares, round_a, round_b)
    squares = exchange_sum(exchange_sum(squares, "core", 2, 1), "z", N_Z, 1)
    first_i[0] = after(first_i[0], squares)
    second_a, second_b, squares = multiply(first_j, first_i, squares, True)

    scale = math.sqrt(R * C) / (jnp.sqrt(squares[0, 0]) + 1e-07)
    start_iterate = new_momentum * scale
    first_product = jnp.concatenate([first_a, first_b], axis=1)
    second_product = jnp.concatenate([second_a, second_b], axis=1)
    update = 0.2 * (
        quintic_a * iterate.astype(jnp.float32)
        + quintic_b * first_product
        + quintic_c * second_product
    )
    return (new_momentum, start_iterate, update)


def solution(mesh):
    fine = Mesh(mesh.devices.reshape(N_DP, N_ROW, N_Z, 2), ("dp", "row", "z", "core"))
    in_specs = (
        P("dp", "row", ("z", "core")),
        P("row", "dp", ("z", "core")),
        P(("dp", "row"), ("z", "core")),
    )
    out_specs = (in_specs[1], in_specs[1], in_specs[2])
    return jax.shard_map(local, mesh=fine, in_specs=in_specs, out_specs=out_specs, check_vma=False)
```

```python
import math

import jax
import jax.numpy as jnp
from jax import lax
from jax.sharding import Mesh
from jax.sharding import PartitionSpec as P

R = 7168
C = 8192

quintic_a = 3.4445
quintic_b = -4.775
quintic_c = 2.0315

N_DP = 4
N_ROW = 4
N_Z = 8
HALF = 256
contract_last = (((1,), (1,)), ((), ()))
contract_first = (((0,), (0,)), ((), ()))
contract_plain = (((1,), (0,)), ((), ()))


def fetch(value, axis, size, offset):
    return lax.ppermute(value, axis, [((i + offset) % size, i) for i in range(size)])


def swap_cores(value):
    return lax.ppermute(value, "core", [(0, 1), (1, 0)])


def dot(left, right, dims):
    return lax.dot_general(left, right, dims, preferred_element_type=jnp.float32)


EXTRA = 16


def with_number(block, number):
    high = lax.reduce_precision(number, 8, 7)
    middle = lax.reduce_precision(number - high, 8, 7)
    rows = jnp.concatenate([high, middle, number - high - middle], axis=0).astype(jnp.bfloat16)
    rows = jnp.pad(rows, ((0, EXTRA - 3), (0, block.shape[1] - rows.shape[1])))
    return jnp.concatenate([block, rows], axis=0)


def numbers_sum(values):
    total = values[0][-EXTRA:, :128].astype(jnp.float32)
    for value in values[1:]:
        total = total + value[-EXTRA:, :128].astype(jnp.float32)
    return jnp.sum(total, axis=0, keepdims=True)


def after(value, *others):
    return lax.optimization_barrier((value,) + others)[0]


def gather_two_ways(value, axis):
    half = value.shape[0] // 2
    ahead = fetch(value, axis, 4, 1)
    behind = fetch(value, axis, 4, -1)
    top = fetch(ahead[:half], axis, 4, 1)
    bottom = fetch(behind[half:], axis, 4, -1)
    return [value, ahead, jnp.concatenate([top, bottom], axis=0), behind]


def local(grad_parts, momentum, iterate):
    core = lax.axis_index("core")
    place_z = lax.axis_index("z")
    height = iterate.shape[0]
    shard = 4 * height // N_Z
    inverse_width = 1.0 / C

    def by_core(for_first, for_second):
        return jnp.where(core == 0, for_first, for_second)

    def stack(blocks):
        return jnp.concatenate(blocks, axis=0)

    def own_half(blocks):
        return stack([by_core(blocks[1], blocks[3]), by_core(blocks[0], blocks[2])])

    def other_half(blocks):
        return stack([by_core(blocks[3], blocks[1]), by_core(blocks[2], blocks[0])])

    blocks_i = gather_two_ways(iterate, "row")
    blocks_j = gather_two_ways(iterate, "dp")
    rows_i, rows_i_other = stack(blocks_i), stack([swap_cores(block) for block in blocks_i])
    rows_j = own_half(blocks_j)
    rows_j_other = stack(
        [
            swap_cores(by_core(blocks_j[3], blocks_j[1])),
            swap_cores(by_core(blocks_j[2], blocks_j[0])),
        ]
    )
    def place(offset):
        return lax.rem(place_z + (offset + N_Z), N_Z) * shard

    def rows_of_shard(offset, arrived=()):
        own = lax.dynamic_slice_in_dim(rows_i, place(offset), shard, 0)
        other = lax.dynamic_slice_in_dim(rows_i_other, place(offset), shard, 0)
        own, other = after(own, *arrived), after(other, *arrived)
        part = dot(own, rows_j, contract_last) + dot(other, rows_j_other, contract_last)
        return lax.optimization_barrier(part * inverse_width)

    def up(value):
        return fetch(value, "z", N_Z, -1)

    def down(value):
        return fetch(value, "z", N_Z, 1)

    half = shard // 2
    opposite = rows_of_shard(4).astype(jnp.bfloat16)

    place_dp = lax.axis_index("dp")
    rows_of = [
        lax.dynamic_slice_in_dim(grad_parts, lax.rem(place_dp + k, N_DP) * height, height, 1)
        for k in range(N_DP)
    ]

    def from_dp(k, rows, *others):
        return fetch(after(rows_of[k][:, rows], *others), "dp", N_DP, -k).astype(jnp.float32)

    above, below = slice(0, height // 2), slice(height // 2, height)
    one = fetch(after(rows_of[1], blocks_j[2]), "dp", N_DP, -1)
    opposite, one = lax.optimization_barrier((opposite, one))
    summed = rows_of[0].astype(jnp.float32) + one.astype(jnp.float32)
    sums = {0: summed[:, above], 1: summed[:, below]}
    rising, falling = up(opposite[:half]), down(opposite[half:])
    arrived = ()
    zeros = jnp.zeros((half, 2 * height), jnp.float32)
    after_first = (rising, falling)
    rising = stack([rising.astype(jnp.float32), zeros])
    falling = stack([zeros, falling.astype(jnp.float32)])
    halves = {0: above, 1: below}
    for offset, wanted in ((3, ((3, 0),)), (2, ((3, 1), (2, 0))), (1, ((2, 1),))):
        rising, falling = lax.optimization_barrier(
            (
                (rows_of_shard(offset, arrived) + rising).astype(jnp.bfloat16),
                (rows_of_shard(-offset, arrived) + falling).astype(jnp.bfloat16),
            )
        )
        partial_sums = [from_dp(k, halves[part], rising) for k, part in wanted]
        rising, falling, *partial_sums = lax.optimization_barrier(
            (up(rising), down(falling), *partial_sums)
        )
        for (_, part), value in zip(wanted, partial_sums):
            sums[part] = sums[part] + value
        arrived, after_first = after_first, (rising, falling)
        rising, falling = rising.astype(jnp.float32), falling.astype(jnp.float32)
    share = (rows_of_shard(0, arrived) + rising + falling).astype(jnp.bfloat16)
    new_momentum = [0.95 * momentum[:, halves[part]] + sums[part] for part in (0, 1)]
    squares = [
        jnp.sum((value * value).reshape(-1, 4, 128), axis=(0, 1)).reshape(1, 128)
        for value in new_momentum
    ]
    new_momentum = jnp.concatenate(new_momentum, axis=1)
    share = with_number(share, squares[0] + squares[1])

    gram_mine = jnp.zeros((4 * height, 2 * height), jnp.bfloat16)
    gram_other = jnp.zeros((4 * height, 2 * height), jnp.bfloat16)

    def put(value, begin):
        swapped = swap_cores(value)
        height = shard if value.shape[0] > shard else value.shape[0]
        return (
            lax.dynamic_update_slice_in_dim(gram_mine, value[:height], begin, 0),
            lax.dynamic_update_slice_in_dim(gram_other, swapped[:height], begin, 0),
            [value, swapped],
        )

    gram_mine, gram_other, carried = put(share, place(0))
    rising = falling = share
    for step in (1, 2, 3):
        rising, falling = lax.optimization_barrier((up(rising), down(falling)))
        gram_mine, gram_other, more = put(rising, place(-step))
        carried += more
        gram_mine, gram_other, more = put(falling, place(step))
        carried += more
    opposite = stack([up(rising[:half]), down(falling[half:])])
    gram_mine, gram_other, more = put(opposite, place(4))
    squares = numbers_sum(carried + more)

    def multiply(of_j, of_i, squares=None):
        part_i = dot(gram_mine, own_half(of_j), contract_plain) + dot(
            gram_other, other_half(of_j), contract_plain
        )
        sent_i = []
        for k in (1, 2, 3):
            block = part_i[k * height : (k + 1) * height].astype(jnp.bfloat16)
            if squares is not None:
                block = with_number(block, squares)
            sent_i.append(fetch(block, "row", N_ROW, -k))
        rows_i = stack(of_i)
        mine = dot(gram_mine, rows_i, contract_first)
        other = dot(gram_other, rows_i, contract_first)
        part_j = {
            0: by_core(mine[height:], other[height:]),
            1: by_core(mine[:height], other[:height]),
            2: by_core(other[height:], mine[height:]),
            3: by_core(other[:height], mine[:height]),
        }
        sent_j = [fetch(part_j[k].astype(jnp.bfloat16), "dp", N_DP, -k) for k in (1, 2, 3)]
        sum_i, sum_j = part_i[:height], part_j[0]
        for got_i, got_j in zip(sent_i, sent_j):
            sum_i = sum_i + got_i[:height].astype(jnp.float32)
            sum_j = sum_j + got_j.astype(jnp.float32)
        if squares is not None:
            squares = squares + numbers_sum(sent_i)
        return sum_i, sum_j, squares

    first_a, first_b, squares = multiply(
        [block[:, :HALF] for block in blocks_j],
        [block[:, HALF:] for block in blocks_i],
        squares,
    )
    round_a, round_b = first_a.astype(jnp.bfloat16), first_b.astype(jnp.bfloat16)
    carrying = with_number(round_a, squares)
    first_j = [carrying] + [fetch(carrying, "dp", N_DP, k) for k in (1, 2, 3)]
    squares = numbers_sum(first_j)
    first_j = [block[:height] for block in first_j]
    first_i = [round_b] + [fetch(round_b, "row", N_ROW, k) for k in (1, 2, 3)]
    second_a, second_b, _ = multiply(first_j, first_i)

    scale = math.sqrt(R * C) / (jnp.sqrt(jnp.sum(squares)) + 1e-07)
    start_iterate = new_momentum * scale
    first_product = jnp.concatenate([first_a, first_b], axis=1)
    second_product = jnp.concatenate([second_a, second_b], axis=1)
    update = 0.2 * (
        quintic_a * iterate.astype(jnp.float32)
        + quintic_b * first_product
        + quintic_c * second_product
    )
    return (new_momentum, start_iterate, update)


def solution(mesh):
    fine = Mesh(mesh.devices.reshape(N_DP, N_ROW, N_Z, 2), ("dp", "row", "z", "core"))
    in_specs = (
        P("dp", "row", ("z", "core")),
        P("row", "dp", ("z", "core")),
        P(("dp", "row"), ("z", "core")),
    )
    out_specs = (in_specs[1], in_specs[1], in_specs[2])
    return jax.shard_map(local, mesh=fine, in_specs=in_specs, out_specs=out_specs, check_vma=False)
```

```python
import math

import jax
import jax.numpy as jnp
from jax import lax
from jax.sharding import Mesh
from jax.sharding import PartitionSpec as P

R = 7168
C = 8192

quintic_a = 3.4445
quintic_b = -4.775
quintic_c = 2.0315

N_DP = 4
N_ROW = 4
N_Z = 8
HALF = 256
contract_last = (((1,), (1,)), ((), ()))
contract_first = (((0,), (0,)), ((), ()))
contract_plain = (((1,), (0,)), ((), ()))


def fetch(value, axis, size, offset):
    return lax.ppermute(value, axis, [((i + offset) % size, i) for i in range(size)])


def swap_cores(value):
    return lax.ppermute(value, "core", [(0, 1), (1, 0)])


def dot(left, right, dims):
    return lax.dot_general(left, right, dims, preferred_element_type=jnp.float32)


EXTRA = 16


def with_number(block, number):
    high = lax.reduce_precision(number, 8, 7)
    middle = lax.reduce_precision(number - high, 8, 7)
    rows = jnp.concatenate([high, middle, number - high - middle], axis=0).astype(jnp.bfloat16)
    rows = jnp.pad(rows, ((0, EXTRA - 3), (0, block.shape[1] - rows.shape[1])))
    return jnp.concatenate([block, rows], axis=0)


def numbers_sum(values):
    total = values[0][-EXTRA:, :128].astype(jnp.float32)
    for value in values[1:]:
        total = total + value[-EXTRA:, :128].astype(jnp.float32)
    return jnp.sum(total, axis=0, keepdims=True)


def after(value, *others):
    return lax.optimization_barrier((value,) + others)[0]


def gather_two_ways(value, axis):
    half = value.shape[0] // 2
    ahead = fetch(value, axis, 4, 1)
    behind = fetch(value, axis, 4, -1)
    top = fetch(ahead[:half], axis, 4, 1)
    bottom = fetch(behind[half:], axis, 4, -1)
    return [value, ahead, jnp.concatenate([top, bottom], axis=0), behind]


def local(grad_parts, momentum, iterate):
    core = lax.axis_index("core")
    place_z = lax.axis_index("z")
    height = iterate.shape[0]
    shard = 4 * height // N_Z
    inverse_width = 1.0 / C

    def by_core(for_first, for_second):
        return jnp.where(core == 0, for_first, for_second)

    def stack(blocks):
        return jnp.concatenate(blocks, axis=0)

    def own_half(blocks):
        return stack([by_core(blocks[1], blocks[3]), by_core(blocks[0], blocks[2])])

    def other_half(blocks):
        return stack([by_core(blocks[3], blocks[1]), by_core(blocks[2], blocks[0])])

    blocks_i = gather_two_ways(iterate, "row")
    blocks_j = gather_two_ways(iterate, "dp")
    rows_i, rows_i_other = stack(blocks_i), stack([swap_cores(block) for block in blocks_i])
    rows_j = own_half(blocks_j)
    rows_j_other = stack(
        [
            swap_cores(by_core(blocks_j[3], blocks_j[1])),
            swap_cores(by_core(blocks_j[2], blocks_j[0])),
        ]
    )
    def place(offset):
        return lax.rem(place_z + (offset + N_Z), N_Z) * shard

    def rows_of_shard(offset, arrived=()):
        own = lax.dynamic_slice_in_dim(rows_i, place(offset), shard, 0)
        other = lax.dynamic_slice_in_dim(rows_i_other, place(offset), shard, 0)
        own, other = after(own, *arrived), after(other, *arrived)
        part = dot(own, rows_j, contract_last) + dot(other, rows_j_other, contract_last)
        return lax.optimization_barrier(part * inverse_width)

    def up(value):
        return fetch(value, "z", N_Z, -1)

    def down(value):
        return fetch(value, "z", N_Z, 1)

    half = shard // 2
    opposite = rows_of_shard(4).astype(jnp.bfloat16)

    place_dp = lax.axis_index("dp")
    rows_of = [
        lax.dynamic_slice_in_dim(grad_parts, lax.rem(place_dp + k, N_DP) * height, height, 1)
        for k in range(N_DP)
    ]

    def from_dp(k, rows, *others):
        return fetch(after(rows_of[k][:, rows], *others), "dp", N_DP, -k).astype(jnp.float32)

    above, below = slice(0, height // 2), slice(height // 2, height)
    sums = {0: rows_of[0][:, above].astype(jnp.float32), 1: rows_of[0][:, below].astype(jnp.float32)}
    opposite, *rows_of = lax.optimization_barrier((opposite, *rows_of))
    rising, falling = up(opposite[:half]), down(opposite[half:])
    arrived = ()
    zeros = jnp.zeros((half, 2 * height), jnp.float32)
    halves = {0: above, 1: below}
    partial_sums = [from_dp(1, above), from_dp(3, above)]
    rising, falling, *partial_sums = lax.optimization_barrier((rising, falling, *partial_sums))
    sums[0] = sums[0] + partial_sums[0] + partial_sums[1]
    after_first = (rising, falling)
    rising = stack([rising.astype(jnp.float32), zeros])
    falling = stack([zeros, falling.astype(jnp.float32)])
    for offset, wanted in ((3, ((1, 1), (3, 1))), (2, ((2, 0),)), (1, ((2, 1),))):
        rising = (rows_of_shard(offset, arrived[:1]) + rising).astype(jnp.bfloat16)
        falling = (rows_of_shard(-offset, arrived[1:]) + falling).astype(jnp.bfloat16)
        partial_sums = [from_dp(k, halves[part], rising, falling) for k, part in wanted]
        rising, falling = up(rising), down(falling)
        rising, *partial_sums = lax.optimization_barrier((rising, *partial_sums))
        for (_, part), value in zip(wanted, partial_sums):
            sums[part] = sums[part] + value
        arrived, after_first = after_first, (rising, falling)
        rising, falling = rising.astype(jnp.float32), falling.astype(jnp.float32)
    share = (rows_of_shard(0, arrived) + rising + falling).astype(jnp.bfloat16)
    new_momentum = [0.95 * momentum[:, halves[part]] + sums[part] for part in (0, 1)]
    squares = [
        jnp.sum((value * value).reshape(-1, 4, 128), axis=(0, 1)).reshape(1, 128)
        for value in new_momentum
    ]
    new_momentum = jnp.concatenate(new_momentum, axis=1)
    share = with_number(share, squares[0] + squares[1])

    gram_mine = jnp.zeros((4 * height, 2 * height), jnp.bfloat16)
    gram_other = jnp.zeros((4 * height, 2 * height), jnp.bfloat16)

    def put(value, begin):
        swapped = swap_cores(value)
        height = shard if value.shape[0] > shard else value.shape[0]
        return (
            lax.dynamic_update_slice_in_dim(gram_mine, value[:height], begin, 0),
            lax.dynamic_update_slice_in_dim(gram_other, swapped[:height], begin, 0),
            [value, swapped],
        )

    gram_mine, gram_other, carried = put(share, place(0))
    rising = falling = share
    for step in (1, 2, 3):
        rising, falling = up(rising), down(falling)
        gram_mine, gram_other, more = put(rising, place(-step))
        carried += more
        gram_mine, gram_other, more = put(falling, place(step))
        carried += more
    opposite = stack([up(rising[:half]), down(falling[half:])])
    gram_mine, gram_other, more = put(opposite, place(4))
    squares = numbers_sum(carried + more)

    def multiply(of_j, of_i, squares=None):
        part_i = dot(gram_mine, own_half(of_j), contract_plain) + dot(
            gram_other, other_half(of_j), contract_plain
        )
        sent_i = []
        for k in (1, 2, 3):
            block = part_i[k * height : (k + 1) * height].astype(jnp.bfloat16)
            if squares is not None:
                block = with_number(block, squares)
            sent_i.append(fetch(block, "row", N_ROW, -k))
        rows_i = stack(of_i)
        mine = dot(gram_mine, rows_i, contract_first)
        other = dot(gram_other, rows_i, contract_first)
        part_j = {
            0: by_core(mine[height:], other[height:]),
            1: by_core(mine[:height], other[:height]),
            2: by_core(other[height:], mine[height:]),
            3: by_core(other[:height], mine[:height]),
        }
        sent_j = [fetch(part_j[k].astype(jnp.bfloat16), "dp", N_DP, -k) for k in (1, 2, 3)]
        sum_i, sum_j = part_i[:height], part_j[0]
        for got_i, got_j in zip(sent_i, sent_j):
            sum_i = sum_i + got_i[:height].astype(jnp.float32)
            sum_j = sum_j + got_j.astype(jnp.float32)
        if squares is not None:
            squares = squares + numbers_sum(sent_i)
        return sum_i, sum_j, squares

    first_a, first_b, squares = multiply(
        [block[:, :HALF] for block in blocks_j],
        [block[:, HALF:] for block in blocks_i],
        squares,
    )
    round_a, round_b = first_a.astype(jnp.bfloat16), first_b.astype(jnp.bfloat16)
    carrying = with_number(round_a, squares)
    first_j = [carrying] + [fetch(carrying, "dp", N_DP, k) for k in (1, 2, 3)]
    squares = numbers_sum(first_j)
    first_j = [block[:height] for block in first_j]
    first_i = [round_b] + [fetch(round_b, "row", N_ROW, k) for k in (1, 2, 3)]
    second_a, second_b, _ = multiply(first_j, first_i)

    scale = math.sqrt(R * C) / (jnp.sqrt(jnp.sum(squares)) + 1e-07)
    start_iterate = new_momentum * scale
    first_product = jnp.concatenate([first_a, first_b], axis=1)
    second_product = jnp.concatenate([second_a, second_b], axis=1)
    update = 0.2 * (
        quintic_a * iterate.astype(jnp.float32)
        + quintic_b * first_product
        + quintic_c * second_product
    )
    return (new_momentum, start_iterate, update)


def solution(mesh):
    fine = Mesh(mesh.devices.reshape(N_DP, N_ROW, N_Z, 2), ("dp", "row", "z", "core"))
    in_specs = (
        P("dp", "row", ("z", "core")),
        P("row", "dp", ("z", "core")),
        P(("dp", "row"), ("z", "core")),
    )
    out_specs = (in_specs[1], in_specs[1], in_specs[2])
    return jax.shard_map(local, mesh=fine, in_specs=in_specs, out_specs=out_specs, check_vma=False)
```

```python
import math

import jax
import jax.numpy as jnp
from jax import lax
from jax.sharding import Mesh
from jax.sharding import PartitionSpec as P

R = 7168
C = 8192

quintic_a = 3.4445
quintic_b = -4.775
quintic_c = 2.0315

N_DP = 4
N_ROW = 4
N_Z = 8
HALF = 256
contract_last = (((1,), (1,)), ((), ()))
contract_first = (((0,), (0,)), ((), ()))
contract_plain = (((1,), (0,)), ((), ()))


def fetch(value, axis, size, offset):
    return lax.ppermute(value, axis, [((i + offset) % size, i) for i in range(size)])


def swap_cores(value):
    return lax.ppermute(value, "core", [(0, 1), (1, 0)])


def dot(left, right, dims):
    return lax.dot_general(left, right, dims, preferred_element_type=jnp.float32)


EXTRA = 16


def with_number(block, number):
    high = lax.reduce_precision(number, 8, 7)
    middle = lax.reduce_precision(number - high, 8, 7)
    rows = jnp.concatenate([high, middle, number - high - middle], axis=0).astype(jnp.bfloat16)
    rows = jnp.pad(rows, ((0, EXTRA - 3), (0, block.shape[1] - rows.shape[1])))
    return jnp.concatenate([block, rows], axis=0)


def numbers_sum(values):
    total = values[0][-EXTRA:, :128].astype(jnp.float32)
    for value in values[1:]:
        total = total + value[-EXTRA:, :128].astype(jnp.float32)
    return jnp.sum(total, axis=0, keepdims=True)


def after(value, *others):
    return lax.optimization_barrier((value,) + others)[0]


def gather_two_ways(value, axis):
    half = value.shape[0] // 2
    ahead = fetch(value, axis, 4, 1)
    behind = fetch(value, axis, 4, -1)
    top = fetch(ahead[:half], axis, 4, 1)
    bottom = fetch(behind[half:], axis, 4, -1)
    return [value, ahead, jnp.concatenate([top, bottom], axis=0), behind]


def local(grad_parts, momentum, iterate):
    core = lax.axis_index("core")
    place_z = lax.axis_index("z")
    height = iterate.shape[0]
    shard = 4 * height // N_Z
    inverse_width = 1.0 / C

    def by_core(for_first, for_second):
        return jnp.where(core == 0, for_first, for_second)

    def stack(blocks):
        return jnp.concatenate(blocks, axis=0)

    def own_half(blocks):
        return stack([by_core(blocks[1], blocks[3]), by_core(blocks[0], blocks[2])])

    def other_half(blocks):
        return stack([by_core(blocks[3], blocks[1]), by_core(blocks[2], blocks[0])])

    blocks_i = gather_two_ways(iterate, "row")
    blocks_j = gather_two_ways(iterate, "dp")
    rows_i, rows_i_other = stack(blocks_i), stack([swap_cores(block) for block in blocks_i])
    rows_j = own_half(blocks_j)
    rows_j_other = stack(
        [
            swap_cores(by_core(blocks_j[3], blocks_j[1])),
            swap_cores(by_core(blocks_j[2], blocks_j[0])),
        ]
    )
    def place(offset):
        return lax.rem(place_z + (offset + N_Z), N_Z) * shard

    def rows_of_shard(offset, arrived=()):
        own = lax.dynamic_slice_in_dim(rows_i, place(offset), shard, 0)
        other = lax.dynamic_slice_in_dim(rows_i_other, place(offset), shard, 0)
        own, other = after(own, *arrived), after(other, *arrived)
        part = dot(own, rows_j, contract_last) + dot(other, rows_j_other, contract_last)
        return lax.optimization_barrier(part * inverse_width)

    def up(value):
        return fetch(value, "z", N_Z, -1)

    def down(value):
        return fetch(value, "z", N_Z, 1)

    half = shard // 2
    opposite = rows_of_shard(4).astype(jnp.bfloat16)

    place_dp = lax.axis_index("dp")
    rows_of = [
        lax.dynamic_slice_in_dim(grad_parts, lax.rem(place_dp + k, N_DP) * height, height, 1)
        for k in range(N_DP)
    ]

    above, below = slice(0, height // 2), slice(height // 2, height)
    opposite, *rows_of = lax.optimization_barrier((opposite, *rows_of))
    rising, falling = up(opposite[:half]), down(opposite[half:])
    zeros = jnp.zeros((half, 2 * height), jnp.float32)

    def to_behind(value, *others):
        return fetch(after(value, *others), "dp", N_DP, 1)

    def to_ahead(value, *others):
        return fetch(after(value, *others), "dp", N_DP, -1)

    def joined(rows, far):
        total = rows_of[3][:, rows].astype(jnp.float32) + far.astype(jnp.float32)
        return total.astype(jnp.bfloat16)

    far_above = to_behind(rows_of[2][:, above])
    rising, falling, far_above = lax.optimization_barrier((rising, falling, far_above))
    arrived = ()
    after_first = (rising, falling)
    rising = stack([rising.astype(jnp.float32), zeros])
    falling = stack([zeros, falling.astype(jnp.float32)])
    for offset in (3, 2, 1):
        rising = (rows_of_shard(offset, arrived[:1]) + rising).astype(jnp.bfloat16)
        falling = (rows_of_shard(-offset, arrived[1:]) + falling).astype(jnp.bfloat16)
        if offset == 3:
            beside = [
                to_behind(rows_of[2][:, below], rising, falling),
                to_ahead(rows_of[1][:, above], rising, falling),
            ]
        elif offset == 2:
            far_below, one_above = beside
            beside = [
                to_behind(joined(above, far_above), rising, falling),
                to_ahead(rows_of[1][:, below], rising, falling),
            ]
        else:
            joined_above, one_below = beside
            beside = [to_behind(joined(below, far_below), rising, falling)]
        rising, falling = up(rising), down(falling)
        rising, *beside = lax.optimization_barrier((rising, *beside))
        arrived, after_first = after_first, (rising, falling)
        rising, falling = rising.astype(jnp.float32), falling.astype(jnp.float32)
    sums = [
        rows_of[0][:, rows].astype(jnp.float32) + one.astype(jnp.float32) + two.astype(jnp.float32)
        for rows, one, two in ((above, one_above, joined_above), (below, one_below, beside[0]))
    ]
    share = (rows_of_shard(0, arrived) + rising + falling).astype(jnp.bfloat16)
    new_momentum = [0.95 * momentum[:, rows] + part for rows, part in zip((above, below), sums)]
    squares = [
        jnp.sum((value * value).reshape(-1, 4, 128), axis=(0, 1)).reshape(1, 128)
        for value in new_momentum
    ]
    new_momentum = jnp.concatenate(new_momentum, axis=1)
    share = with_number(share, squares[0] + squares[1])

    gram_mine = jnp.zeros((4 * height, 2 * height), jnp.bfloat16)
    gram_other = jnp.zeros((4 * height, 2 * height), jnp.bfloat16)

    def put(value, begin):
        swapped = swap_cores(value)
        height = shard if value.shape[0] > shard else value.shape[0]
        return (
            lax.dynamic_update_slice_in_dim(gram_mine, value[:height], begin, 0),
            lax.dynamic_update_slice_in_dim(gram_other, swapped[:height], begin, 0),
            [value, swapped],
        )

    gram_mine, gram_other, carried = put(share, place(0))
    rising = falling = share
    for step in (1, 2, 3):
        rising, falling = up(rising), down(falling)
        gram_mine, gram_other, more = put(rising, place(-step))
        carried += more
        gram_mine, gram_other, more = put(falling, place(step))
        carried += more
    opposite = stack([up(rising[:half]), down(falling[half:])])
    gram_mine, gram_other, more = put(opposite, place(4))
    squares = numbers_sum(carried + more)

    def sum_blocks(blocks, axis, number=None):
        def packed(block, number):
            block = block.astype(jnp.bfloat16)
            return block if number is None else with_number(block, number)

        far = fetch(packed(blocks[2], number), axis, 4, 1)
        ahead = fetch(packed(blocks[1], number), axis, 4, -1)
        joined = blocks[3] + far[:height].astype(jnp.float32)
        both = None if number is None else number + numbers_sum([far])
        behind = fetch(packed(joined, both), axis, 4, 1)
        total = blocks[0] + ahead[:height].astype(jnp.float32) + behind[:height].astype(jnp.float32)
        return total, None if number is None else number + numbers_sum([ahead, behind])

    def multiply(of_j, of_i, number=None):
        rows_i = stack(of_i)
        mine = dot(gram_mine, rows_i, contract_first)
        other = dot(gram_other, rows_i, contract_first)
        part_j = [
            by_core(mine[height:], other[height:]),
            by_core(mine[:height], other[:height]),
            by_core(other[height:], mine[height:]),
            by_core(other[:height], mine[:height]),
        ]
        sum_j, _ = sum_blocks(part_j, "dp")
        part_i = dot(gram_mine, own_half(of_j), contract_plain) + dot(
            gram_other, other_half(of_j), contract_plain
        )
        part_i = [part_i[k * height : (k + 1) * height] for k in range(4)]
        sum_i, number = sum_blocks(part_i, "row", number)
        return sum_i, sum_j, number

    def gather_blocks(value, axis):
        ahead = fetch(value, axis, 4, 1)
        behind = fetch(value, axis, 4, -1)
        return [value, ahead, fetch(ahead, axis, 4, 1), behind]

    first_a, first_b, squares = multiply(
        [block[:, :HALF] for block in blocks_j],
        [block[:, HALF:] for block in blocks_i],
        squares,
    )
    round_a, round_b = first_a.astype(jnp.bfloat16), first_b.astype(jnp.bfloat16)
    carrying = with_number(round_a, squares)
    first_j = gather_blocks(carrying, "dp")
    squares = numbers_sum(first_j)
    first_j = [block[:height] for block in first_j]
    first_i = gather_blocks(round_b, "row")
    second_a, second_b, _ = multiply(first_j, first_i)

    scale = math.sqrt(R * C) / (jnp.sqrt(jnp.sum(squares)) + 1e-07)
    start_iterate = new_momentum * scale
    first_product = jnp.concatenate([first_a, first_b], axis=1)
    second_product = jnp.concatenate([second_a, second_b], axis=1)
    update = 0.2 * (
        quintic_a * iterate.astype(jnp.float32)
        + quintic_b * first_product
        + quintic_c * second_product
    )
    return (new_momentum, start_iterate, update)


def solution(mesh):
    fine = Mesh(mesh.devices.reshape(N_DP, N_ROW, N_Z, 2), ("dp", "row", "z", "core"))
    in_specs = (
        P("dp", "row", ("z", "core")),
        P("row", "dp", ("z", "core")),
        P(("dp", "row"), ("z", "core")),
    )
    out_specs = (in_specs[1], in_specs[1], in_specs[2])
    return jax.shard_map(local, mesh=fine, in_specs=in_specs, out_specs=out_specs, check_vma=False)
```

```python
import math

import jax
import jax.numpy as jnp
from jax import lax
from jax.sharding import Mesh
from jax.sharding import PartitionSpec as P

R = 7168
C = 8192

quintic_a = 3.4445
quintic_b = -4.775
quintic_c = 2.0315

N_DP = 4
N_ROW = 4
N_Z = 8
HALF = 256
contract_last = (((1,), (1,)), ((), ()))
contract_first = (((0,), (0,)), ((), ()))
contract_plain = (((1,), (0,)), ((), ()))


def fetch(value, axis, size, offset):
    return lax.ppermute(value, axis, [((i + offset) % size, i) for i in range(size)])


def swap_cores(value):
    return lax.ppermute(value, "core", [(0, 1), (1, 0)])


def dot(left, right, dims):
    return lax.dot_general(left, right, dims, preferred_element_type=jnp.float32)


EXTRA = 16


def with_number(block, number):
    high = lax.reduce_precision(number, 8, 7)
    middle = lax.reduce_precision(number - high, 8, 7)
    rows = jnp.concatenate([high, middle, number - high - middle], axis=0).astype(jnp.bfloat16)
    rows = jnp.pad(rows, ((0, EXTRA - 3), (0, block.shape[1] - rows.shape[1])))
    return jnp.concatenate([block, rows], axis=0)


def numbers_sum(values):
    total = values[0][-EXTRA:, :128].astype(jnp.float32)
    for value in values[1:]:
        total = total + value[-EXTRA:, :128].astype(jnp.float32)
    return jnp.sum(total, axis=0, keepdims=True)


def after(value, *others):
    return lax.optimization_barrier((value,) + others)[0]


def gather_two_ways(value, axis):
    half = value.shape[0] // 2
    ahead = fetch(value, axis, 4, 1)
    behind = fetch(value, axis, 4, -1)
    top = fetch(ahead[:half], axis, 4, 1)
    bottom = fetch(behind[half:], axis, 4, -1)
    return [value, ahead, jnp.concatenate([top, bottom], axis=0), behind]


def local(grad_parts, momentum, iterate):
    core = lax.axis_index("core")
    place_z = lax.axis_index("z")
    height = iterate.shape[0]
    shard = 4 * height // N_Z
    inverse_width = 1.0 / C

    def by_core(for_first, for_second):
        return jnp.where(core == 0, for_first, for_second)

    def stack(blocks):
        return jnp.concatenate(blocks, axis=0)

    def own_half(blocks):
        return stack([by_core(blocks[1], blocks[3]), by_core(blocks[0], blocks[2])])

    def other_half(blocks):
        return stack([by_core(blocks[3], blocks[1]), by_core(blocks[2], blocks[0])])

    blocks_i = gather_two_ways(iterate, "row")
    blocks_j = gather_two_ways(iterate, "dp")
    rows_i, rows_i_other = stack(blocks_i), stack([swap_cores(block) for block in blocks_i])
    rows_j = own_half(blocks_j)
    rows_j_other = stack(
        [
            swap_cores(by_core(blocks_j[3], blocks_j[1])),
            swap_cores(by_core(blocks_j[2], blocks_j[0])),
        ]
    )
    def place(offset):
        return lax.rem(place_z + (offset + N_Z), N_Z) * shard

    def rows_of_shard(offset, arrived=()):
        own = lax.dynamic_slice_in_dim(rows_i, place(offset), shard, 0)
        other = lax.dynamic_slice_in_dim(rows_i_other, place(offset), shard, 0)
        own, other = after(own, *arrived), after(other, *arrived)
        part = dot(own, rows_j, contract_last) + dot(other, rows_j_other, contract_last)
        return lax.optimization_barrier(part * inverse_width)

    def up(value):
        return fetch(value, "z", N_Z, -1)

    def down(value):
        return fetch(value, "z", N_Z, 1)

    half = shard // 2
    opposite = rows_of_shard(4).astype(jnp.bfloat16)

    place_dp = lax.axis_index("dp")
    rows_of = [
        lax.dynamic_slice_in_dim(grad_parts, lax.rem(place_dp + k, N_DP) * height, height, 1)
        for k in range(N_DP)
    ]

    above, below = slice(0, height // 2), slice(height // 2, height)
    opposite, *rows_of = lax.optimization_barrier((opposite, *rows_of))
    rising, falling = up(opposite[:half]), down(opposite[half:])
    zeros = jnp.zeros((half, 2 * height), jnp.float32)

    def to_behind(value, *others):
        return fetch(after(value, *others), "dp", N_DP, 1)

    def to_ahead(value, *others):
        return fetch(after(value, *others), "dp", N_DP, -1)

    def joined(rows, far):
        total = rows_of[3][:, rows].astype(jnp.float32) + far.astype(jnp.float32)
        return total.astype(jnp.bfloat16)

    far_above = to_behind(rows_of[2][:, above])
    rising, falling, far_above = lax.optimization_barrier((rising, falling, far_above))
    arrived = (opposite, opposite)
    after_first = (rising, falling)
    rising = stack([rising.astype(jnp.float32), zeros])
    falling = stack([zeros, falling.astype(jnp.float32)])
    for offset in (3, 2, 1):
        rising = (rows_of_shard(offset, arrived[:1]) + rising).astype(jnp.bfloat16)
        falling = (rows_of_shard(-offset, arrived[1:]) + falling).astype(jnp.bfloat16)
        if offset == 3:
            beside = [
                to_behind(rows_of[2][:, below], rising, falling),
                to_ahead(rows_of[1][:, above], rising, falling),
            ]
        elif offset == 2:
            far_below, one_above = beside
            beside = [
                to_behind(joined(above, far_above), rising, falling),
                to_ahead(rows_of[1][:, below], rising, falling),
            ]
        else:
            joined_above, one_below = beside
            beside = [to_behind(joined(below, far_below), rising, falling)]
        rising, falling = up(rising), down(falling)
        rising, *beside = lax.optimization_barrier((rising, *beside))
        arrived, after_first = after_first, (rising, falling)
        rising, falling = rising.astype(jnp.float32), falling.astype(jnp.float32)
    sums = [
        rows_of[0][:, rows].astype(jnp.float32) + one.astype(jnp.float32) + two.astype(jnp.float32)
        for rows, one, two in ((above, one_above, joined_above), (below, one_below, beside[0]))
    ]
    share = (rows_of_shard(0, arrived) + rising + falling).astype(jnp.bfloat16)
    new_momentum = [0.95 * momentum[:, rows] + part for rows, part in zip((above, below), sums)]
    squares = [
        jnp.sum((value * value).reshape(-1, 4, 128), axis=(0, 1)).reshape(1, 128)
        for value in new_momentum
    ]
    new_momentum = jnp.concatenate(new_momentum, axis=1)
    share = with_number(share, squares[0] + squares[1])

    gram_mine = jnp.zeros((4 * height, 2 * height), jnp.bfloat16)
    gram_other = jnp.zeros((4 * height, 2 * height), jnp.bfloat16)

    def put(value, begin):
        swapped = swap_cores(value)
        height = shard if value.shape[0] > shard else value.shape[0]
        return (
            lax.dynamic_update_slice_in_dim(gram_mine, value[:height], begin, 0),
            lax.dynamic_update_slice_in_dim(gram_other, swapped[:height], begin, 0),
            [value, swapped],
        )

    gram_mine, gram_other, carried = put(share, place(0))
    rising = falling = share
    for step in (1, 2, 3):
        rising, falling = up(rising), down(falling)
        gram_mine, gram_other, more = put(rising, place(-step))
        carried += more
        gram_mine, gram_other, more = put(falling, place(step))
        carried += more
    opposite = stack([up(rising[:half]), down(falling[half:])])
    gram_mine, gram_other, more = put(opposite, place(4))
    squares = numbers_sum(carried + more)

    def multiply(of_j, of_i, squares=None):
        part_i = dot(gram_mine, own_half(of_j), contract_plain) + dot(
            gram_other, other_half(of_j), contract_plain
        )
        sent_i = []
        for k in (1, 3, 2):
            block = part_i[k * height : (k + 1) * height].astype(jnp.bfloat16)
            if squares is not None:
                block = with_number(block, squares)
            sent_i.append(fetch(block, "row", N_ROW, -k))
        rows_i = stack(of_i)
        mine = dot(gram_mine, rows_i, contract_first)
        other = dot(gram_other, rows_i, contract_first)
        part_j = {
            0: by_core(mine[height:], other[height:]),
            1: by_core(mine[:height], other[:height]),
            2: by_core(other[height:], mine[height:]),
            3: by_core(other[:height], mine[:height]),
        }
        sent_j = [fetch(part_j[k].astype(jnp.bfloat16), "dp", N_DP, -k) for k in (1, 3, 2)]
        sum_i, sum_j = part_i[:height], part_j[0]
        for got_i, got_j in zip(sent_i, sent_j):
            sum_i = sum_i + got_i[:height].astype(jnp.float32)
            sum_j = sum_j + got_j.astype(jnp.float32)
        if squares is not None:
            squares = squares + numbers_sum(sent_i)
        return sum_i, sum_j, squares

    def gather_blocks(value, axis):
        arrived = {k: fetch(value, axis, 4, k) for k in (1, 3, 2)}
        return [value] + [arrived[k] for k in (1, 2, 3)]

    first_a, first_b, squares = multiply(
        [block[:, :HALF] for block in blocks_j],
        [block[:, HALF:] for block in blocks_i],
        squares,
    )
    round_a, round_b = first_a.astype(jnp.bfloat16), first_b.astype(jnp.bfloat16)
    carrying = with_number(round_a, squares)
    first_j = gather_blocks(carrying, "dp")
    squares = numbers_sum(first_j)
    first_j = [block[:height] for block in first_j]
    first_i = gather_blocks(round_b, "row")
    second_a, second_b, _ = multiply(first_j, first_i)

    scale = math.sqrt(R * C) / (jnp.sqrt(jnp.sum(squares)) + 1e-07)
    start_iterate = new_momentum * scale
    first_product = jnp.concatenate([first_a, first_b], axis=1)
    second_product = jnp.concatenate([second_a, second_b], axis=1)
    update = 0.2 * (
        quintic_a * iterate.astype(jnp.float32)
        + quintic_b * first_product
        + quintic_c * second_product
    )
    return (new_momentum, start_iterate, update)


def solution(mesh):
    fine = Mesh(mesh.devices.reshape(N_DP, N_ROW, N_Z, 2), ("dp", "row", "z", "core"))
    in_specs = (
        P("dp", "row", ("z", "core")),
        P("row", "dp", ("z", "core")),
        P(("dp", "row"), ("z", "core")),
    )
    out_specs = (in_specs[1], in_specs[1], in_specs[2])
    return jax.shard_map(local, mesh=fine, in_specs=in_specs, out_specs=out_specs, check_vma=False)
```

```python
import math

import jax
import jax.numpy as jnp
from jax import lax
from jax.sharding import Mesh
from jax.sharding import PartitionSpec as P

R = 7168
C = 8192

quintic_a = 3.4445
quintic_b = -4.775
quintic_c = 2.0315

N_DP = 4
N_ROW = 4
N_Z = 8
HALF = 256
contract_last = (((1,), (1,)), ((), ()))
contract_first = (((0,), (0,)), ((), ()))
contract_plain = (((1,), (0,)), ((), ()))


def fetch(value, axis, size, offset):
    return lax.ppermute(value, axis, [((i + offset) % size, i) for i in range(size)])


def swap_cores(value):
    return lax.ppermute(value, "core", [(0, 1), (1, 0)])


def dot(left, right, dims):
    return lax.dot_general(left, right, dims, preferred_element_type=jnp.float32)


EXTRA = 16


def with_number(block, number):
    high = lax.reduce_precision(number, 8, 7)
    middle = lax.reduce_precision(number - high, 8, 7)
    rows = jnp.concatenate([high, middle, number - high - middle], axis=0).astype(jnp.bfloat16)
    rows = jnp.pad(rows, ((0, EXTRA - 3), (0, block.shape[1] - rows.shape[1])))
    return jnp.concatenate([block, rows], axis=0)


def numbers_sum(values):
    total = values[0][-EXTRA:, :128].astype(jnp.float32)
    for value in values[1:]:
        total = total + value[-EXTRA:, :128].astype(jnp.float32)
    return jnp.sum(total, axis=0, keepdims=True)


def after(value, *others):
    return lax.optimization_barrier((value,) + others)[0]


def gather_two_ways(value, axis):
    half = value.shape[0] // 2
    ahead = fetch(value, axis, 4, 1)
    behind = fetch(value, axis, 4, -1)
    top = fetch(ahead[:half], axis, 4, 1)
    bottom = fetch(behind[half:], axis, 4, -1)
    return [value, ahead, jnp.concatenate([top, bottom], axis=0), behind]


def local(grad_parts, momentum, iterate):
    core = lax.axis_index("core")
    place_z = lax.axis_index("z")
    height = iterate.shape[0]
    shard = 4 * height // N_Z
    inverse_width = 1.0 / C

    def by_core(for_first, for_second):
        return jnp.where(core == 0, for_first, for_second)

    def stack(blocks):
        return jnp.concatenate(blocks, axis=0)

    def own_half(blocks):
        return stack([by_core(blocks[1], blocks[3]), by_core(blocks[0], blocks[2])])

    def other_half(blocks):
        return stack([by_core(blocks[3], blocks[1]), by_core(blocks[2], blocks[0])])

    blocks_i = gather_two_ways(iterate, "row")
    blocks_j = gather_two_ways(iterate, "dp")
    rows_i, rows_i_other = stack(blocks_i), stack([swap_cores(block) for block in blocks_i])
    rows_j = own_half(blocks_j)
    rows_j_other = stack(
        [
            swap_cores(by_core(blocks_j[3], blocks_j[1])),
            swap_cores(by_core(blocks_j[2], blocks_j[0])),
        ]
    )
    def place(offset):
        return lax.rem(place_z + (offset + N_Z), N_Z) * shard

    def rows_of_shard(offset, arrived=()):
        own = lax.dynamic_slice_in_dim(rows_i, place(offset), shard, 0)
        other = lax.dynamic_slice_in_dim(rows_i_other, place(offset), shard, 0)
        own, other = after(own, *arrived), after(other, *arrived)
        part = dot(own, rows_j, contract_last) + dot(other, rows_j_other, contract_last)
        return lax.optimization_barrier(part * inverse_width)

    def up(value):
        return fetch(value, "z", N_Z, -1)

    def down(value):
        return fetch(value, "z", N_Z, 1)

    half = shard // 2
    opposite = rows_of_shard(4).astype(jnp.bfloat16)

    place_dp = lax.axis_index("dp")
    rows_of = [
        lax.dynamic_slice_in_dim(grad_parts, lax.rem(place_dp + k, N_DP) * height, height, 1)
        for k in range(N_DP)
    ]

    above, below = slice(0, height // 2), slice(height // 2, height)
    opposite, *rows_of = lax.optimization_barrier((opposite, *rows_of))
    rising, falling = up(opposite[:half]), down(opposite[half:])
    zeros = jnp.zeros((half, 2 * height), jnp.float32)

    def to_behind(value, *others):
        return fetch(after(value, *others), "dp", N_DP, 1)

    def to_ahead(value, *others):
        return fetch(after(value, *others), "dp", N_DP, -1)

    def joined(rows, far):
        total = rows_of[3][:, rows].astype(jnp.float32) + far.astype(jnp.float32)
        return total.astype(jnp.bfloat16)

    far_above = to_behind(rows_of[2][:, above])
    rising, falling, far_above = lax.optimization_barrier((rising, falling, far_above))
    arrived = ()
    after_first = (rising, falling)
    rising = stack([rising.astype(jnp.float32), zeros])
    falling = stack([zeros, falling.astype(jnp.float32)])
    for offset in (3, 2, 1):
        rising = (rows_of_shard(offset, arrived[:1]) + rising).astype(jnp.bfloat16)
        falling = (rows_of_shard(-offset, arrived[1:]) + falling).astype(jnp.bfloat16)
        if offset == 3:
            beside = [
                to_behind(rows_of[2][:, below], rising, falling),
                to_ahead(rows_of[1][:, above], rising, falling),
            ]
        elif offset == 2:
            far_below, one_above = beside
            beside = [
                to_behind(joined(above, far_above), rising, falling),
                to_ahead(rows_of[1][:, below], rising, falling),
            ]
        else:
            joined_above, one_below = beside
            beside = [to_behind(joined(below, far_below), rising, falling)]
        rising, falling = up(rising), down(falling)
        rising, *beside = lax.optimization_barrier((rising, *beside))
        arrived, after_first = after_first, (rising, falling)
        rising, falling = rising.astype(jnp.float32), falling.astype(jnp.float32)
    sums = [
        rows_of[0][:, rows].astype(jnp.float32) + one.astype(jnp.float32) + two.astype(jnp.float32)
        for rows, one, two in ((above, one_above, joined_above), (below, one_below, beside[0]))
    ]
    share = (rows_of_shard(0, arrived) + rising + falling).astype(jnp.bfloat16)
    new_momentum = [0.95 * momentum[:, rows] + part for rows, part in zip((above, below), sums)]
    squares = [
        jnp.sum((value * value).reshape(-1, 4, 128), axis=(0, 1)).reshape(1, 128)
        for value in new_momentum
    ]
    new_momentum = jnp.concatenate(new_momentum, axis=1)
    share = with_number(share, squares[0] + squares[1])

    gram_mine = jnp.zeros((4 * height, 2 * height), jnp.bfloat16)
    gram_other = jnp.zeros((4 * height, 2 * height), jnp.bfloat16)

    def put(value, begin):
        swapped = swap_cores(value)
        height = shard if value.shape[0] > shard else value.shape[0]
        return (
            lax.dynamic_update_slice_in_dim(gram_mine, value[:height], begin, 0),
            lax.dynamic_update_slice_in_dim(gram_other, swapped[:height], begin, 0),
            [value, swapped],
        )

    gram_mine, gram_other, carried = put(share, place(0))
    rising = falling = share
    for step in (1, 2, 3):
        rising, falling = up(rising), down(falling)
        gram_mine, gram_other, more = put(rising, place(-step))
        carried += more
        gram_mine, gram_other, more = put(falling, place(step))
        carried += more
    opposite = stack([up(rising[:half]), down(falling[half:])])
    gram_mine, gram_other, more = put(opposite, place(4))
    squares = numbers_sum(carried + more)

    def multiply(of_j, of_i, squares=None):
        part_i = dot(gram_mine, own_half(of_j), contract_plain) + dot(
            gram_other, other_half(of_j), contract_plain
        )
        sent_i = []
        for k in (1, 3, 2):
            block = part_i[k * height : (k + 1) * height].astype(jnp.bfloat16)
            if squares is not None:
                block = with_number(block, squares)
            sent_i.append(fetch(block, "row", N_ROW, -k))
        rows_i = stack(of_i)
        mine = dot(gram_mine, rows_i, contract_first)
        other = dot(gram_other, rows_i, contract_first)
        part_j = {
            0: by_core(mine[height:], other[height:]),
            1: by_core(mine[:height], other[:height]),
            2: by_core(other[height:], mine[height:]),
            3: by_core(other[:height], mine[:height]),
        }
        sent_j = [fetch(part_j[k].astype(jnp.bfloat16), "dp", N_DP, -k) for k in (1, 3, 2)]
        sum_i, sum_j = part_i[:height], part_j[0]
        for got_i, got_j in zip(sent_i, sent_j):
            sum_i = sum_i + got_i[:height].astype(jnp.float32)
            sum_j = sum_j + got_j.astype(jnp.float32)
        if squares is not None:
            squares = squares + numbers_sum(sent_i)
        return sum_i, sum_j, squares

    def gather_blocks(value, axis):
        arrived = {k: fetch(value, axis, 4, k) for k in (1, 3, 2)}
        return [value] + [arrived[k] for k in (1, 2, 3)]

    first_a, first_b, squares = multiply(
        [block[:, :HALF] for block in blocks_j],
        [block[:, HALF:] for block in blocks_i],
        squares,
    )
    round_a, round_b = first_a.astype(jnp.bfloat16), first_b.astype(jnp.bfloat16)
    carrying = with_number(round_a, squares)
    first_j = gather_blocks(carrying, "dp")
    squares = numbers_sum(first_j)
    first_j = [block[:height] for block in first_j]
    first_i = gather_blocks(round_b, "row")
    second_a, second_b, _ = multiply(first_j, first_i)

    scale = math.sqrt(R * C) / (jnp.sqrt(jnp.sum(squares)) + 1e-07)
    start_iterate = new_momentum * scale
    first_product = jnp.concatenate([first_a, first_b], axis=1)
    second_product = jnp.concatenate([second_a, second_b], axis=1)
    update = 0.2 * (
        quintic_a * iterate.astype(jnp.float32)
        + quintic_b * first_product
        + quintic_c * second_product
    )
    return (new_momentum, start_iterate, update)


def solution(mesh):
    fine = Mesh(mesh.devices.reshape(N_DP, N_ROW, N_Z, 2), ("dp", "row", "z", "core"))
    in_specs = (
        P("dp", "row", ("z", "core")),
        P("row", "dp", ("z", "core")),
        P(("dp", "row"), ("z", "core")),
    )
    out_specs = (in_specs[1], in_specs[1], in_specs[2])
    return jax.shard_map(local, mesh=fine, in_specs=in_specs, out_specs=out_specs, check_vma=False)
```
